32 devices in a mesh: sx: 4 (over x, core), sy: 4 (over z), depth: 2 (over y).
Axes of the slice: x: 2, y: 2, z: 4, core: 2. Of those that a mesh axis runs over, the one named last changes fastest.
Arguments:
- probe_wave: float32 [2, 128, 128], replicated, may hold values from -4.2 to 4.2
- transmission: float32 [2, 8, 512, 1024], P(None, 'depth', 'sx', 'sy'), may hold values from -0.6 to 0.6
- scan_offsets: int32 [4, 4, 4, 2], P('sx', 'sy'), may hold values from -64 to 192, as said below
- pattern_shifts: int32 [4, 4, 4, 2], P('sx', 'sy'), may hold values from -8 to 8
- patterns: float32 [4, 4, 4, 128, 128], P('sx', 'sy'), may hold values from 0 to 9
Outputs:
- transmission_grad: float32 [2, 8, 512, 1024], P(None, 'depth', 'sx', 'sy')
- probe_grad: float32 [2, 128, 128], replicated
- mean_error: float32 [], replicated
The draws below stay inside these ranges and needn't reach their ends.
Inputs may be any that keep to these rules, and one draw needn't show every extreme that they name: `scan_offsets`: row offsets lie from -64 to 64 and column offsets from -64 to 192; on every scan tile some position takes the smallest and some the largest value of each.
All inputs are finite; a program needn't handle non-finite values.
Results may differ from the reference program's by a relative error of at most 0.0003.
Values sent between devices are 32-bit elements; how exact they have to be, the bound alone decides.
A program may use at most 64 MiB of HBM per device.

```python
import jax
import jax.numpy as jnp
from jax import lax

WIN = 128
POS_DEV = 4
TILE_R = 128
TILE_C = 256
SLABS = 8
HALF = 64
NROW = 512
NCOL = 1024
POSITIONS = 64
N_SX = 4
N_SY = 4


def draw_scan_offsets(key, part):
    keyed = jax.random.fold_in(key, 7)
    first_key, second_key, third_key, fourth_key = jax.random.split(keyed, 4)
    extent = (N_SX, N_SY, POS_DEV)
    row_values = jax.random.randint(first_key, extent, -HALF, TILE_R - HALF + 1)
    col_values = jax.random.randint(second_key, extent, -HALF, TILE_C - HALF + 1)
    lowest = jax.random.randint(third_key, (N_SX, N_SY, 1), 0, POS_DEV)
    offset_step = jax.random.randint(fourth_key, (N_SX, N_SY, 1), 1, POS_DEV)
    highest = (lowest + offset_step) % POS_DEV
    counter = jnp.arange(POS_DEV, dtype=jnp.int32)[None, None, :]
    row_values = jnp.where(counter == lowest, -HALF, row_values)
    row_values = jnp.where(counter == highest, TILE_R - HALF, row_values)
    col_values = jnp.where(counter == lowest, -HALF, col_values)
    col_values = jnp.where(counter == highest, TILE_C - HALF, col_values)
    return jnp.stack([row_values, col_values], axis=-1).astype(jnp.int32)


def draw_patterns(key, part):
    keyed = jax.random.fold_in(key, 11)
    extent = (N_SX, N_SY, POS_DEV, WIN, WIN)
    tile_index = jnp.arange(N_SX * N_SY, dtype=jnp.int32).reshape(N_SX, N_SY, 1, 1, 1).astype(jnp.float32)
    growth = 1.0 + 2.0 * tile_index / max(N_SX * N_SY - 1, 1)
    values = jax.random.uniform(keyed, extent, jnp.float32, 0.0, 2.0)
    return values * growth


def touch_ends(drawn, key, low, top_value):
    shape = drawn.shape
    spot = [jax.random.randint(jax.random.fold_in(key, axis), (), 0, shape[axis]) for axis in range(len(shape))]
    drawn = drawn.at[tuple(spot)].set(low)
    longest = shape.index(max(shape))
    spot[longest] = (spot[longest] + 1) % shape[longest]
    return drawn.at[tuple(spot)].set(top_value)


def steps_of(key, shape, cuts, smallest, top_value):
    factor_of = 1.0
    for axis_at, parts in cuts:
        steps = jax.random.uniform(jax.random.fold_in(jax.random.fold_in(key, 6), axis_at), (parts,), jnp.float32, smallest / len(cuts), top_value / len(cuts))
        factor_of = factor_of * jnp.repeat(jnp.exp(steps), shape[axis_at] // parts).reshape((-1,) + (1,) * (len(shape) - 1 - axis_at))
    return factor_of


def bell_draw(rng, dims, deviation, reach, cuts=(), kind=jnp.bfloat16):
    gain = steps_of(rng, dims, cuts, -0.22, 0.18) if cuts else 1.0
    drawn = jax.random.normal(rng, dims, jnp.float32) * deviation * gain
    return jnp.minimum(jnp.maximum(drawn, -reach), reach).astype(kind)


def setup_inputs(seed: int = 0) -> dict:
    arg_keys = jax.random.split(jax.random.key(seed), 6)
    return {
        "probe_wave": bell_draw(arg_keys[0], (2, WIN, WIN), 0.7, 4.2, (), jnp.float32),
        "transmission": bell_draw(arg_keys[1], (2, SLABS, NROW, NCOL), 0.1, 0.6, ((1, 2), (2, 4), (3, 4)), jnp.float32),
        "scan_offsets": draw_scan_offsets(jax.random.fold_in(arg_keys[5], 71), 0),
        "pattern_shifts": touch_ends(jax.random.randint(arg_keys[3], (N_SX, N_SY, POS_DEV, 2), -8, 9), jax.random.fold_in(arg_keys[3], 1), -8, 8).astype(jnp.int32),
        "patterns": draw_patterns(jax.random.fold_in(arg_keys[5], 71), 0),
    }


FRESNEL = 12.0

def propagate(incoming, kernel):
    return jnp.fft.ifft2(jnp.fft.fft2(incoming) * kernel)

def position_error(windows, probe_wave, measured, shift_pair, kernel):
    current = lax.complex(probe_wave[0], probe_wave[1])
    for slab_number in range(windows.shape[1]):
        factor_layer = lax.complex(1.0 + windows[0, slab_number], windows[1, slab_number])
        current = propagate(current * factor_layer, kernel)
    detector = jnp.fft.fft2(current, norm='ortho')
    intensity = jnp.real(detector) ** 2 + jnp.imag(detector) ** 2
    moved = jnp.roll(intensity, (shift_pair[0], shift_pair[1]), axis=(0, 1))
    residual = moved - measured
    return 0.5 * jnp.sum(residual * residual)

def reference(probe_wave, transmission, scan_offsets, pattern_shifts, patterns):
    border = WIN // 2
    counter = jnp.arange(WIN, dtype=jnp.int32)
    frequency = jnp.where(counter < WIN // 2, counter, counter - WIN).astype(jnp.float32) / WIN
    phases = -FRESNEL * (frequency[:, None] ** 2 + frequency[None, :] ** 2)
    kernel = lax.complex(jnp.cos(phases), jnp.sin(phases))
    grid_rows = jnp.arange(N_SX, dtype=jnp.int32)[:, None, None] * TILE_R
    grid_cols = jnp.arange(N_SY, dtype=jnp.int32)[None, :, None] * TILE_C
    row_starts = (scan_offsets[..., 0] + grid_rows + border).reshape(-1).astype(jnp.int32)
    col_starts = (scan_offsets[..., 1] + grid_cols + border).reshape(-1).astype(jnp.int32)
    shift_table = pattern_shifts.reshape(-1, 2)
    measured_all = patterns.reshape(-1, WIN, WIN)
    padded = jnp.pad(transmission, ((0, 0), (0, 0), (border, border), (border, border)))
    zero_index = jnp.zeros((), jnp.int32)

    def advance(running, inputs):
        gradients, probe_total, error_total = running
        row_start, col_start, shift_pair, measured = inputs
        corner = (zero_index, zero_index, row_start, col_start)
        windows = lax.dynamic_slice(padded, corner, (2, SLABS, WIN, WIN))

        def local_error(window_values, probe_values):
            return position_error(window_values, probe_values, measured, shift_pair, kernel)
        amount, pullback = jax.vjp(local_error, windows, probe_wave)
        window_grad, probe_part = pullback(jnp.ones_like(amount))
        current = lax.dynamic_slice(gradients, corner, (2, SLABS, WIN, WIN))
        gradients = lax.dynamic_update_slice(gradients, current + window_grad, corner)
        return ((gradients, probe_total + probe_part, error_total + amount), None)
    initial = (jnp.zeros(padded.shape, jnp.float32), jnp.zeros((2, WIN, WIN), jnp.float32), jnp.zeros((), jnp.float32))
    final, _ = lax.scan(advance, initial, (row_starts, col_starts, shift_table, measured_all))
    gradients, probe_total, error_total = final
    transmission_grad = gradients[:, :, border:border + NROW, border:border + NCOL]
    return (transmission_grad, probe_total / POSITIONS, error_total / (POSITIONS * WIN * WIN))
```

```python
import functools

import jax
import jax.numpy as jnp
import ml_dtypes
import numpy as np
from jax import lax
from jax.experimental import pallas as pl
from jax.experimental.pallas import tpu as pltpu
from jax.sharding import PartitionSpec as P

FRESNEL = 12.0
F32 = jnp.float32
BF16 = jnp.bfloat16


def split_table(table):
    high = table.astype(np.float32).astype(ml_dtypes.bfloat16)
    low = (table - high.astype(np.float64)).astype(np.float32).astype(ml_dtypes.bfloat16)
    return high, low


def build_tables(points):
    counter = np.arange(points)
    angles = (counter[:, None] * counter[None, :] % points) * (2.0 * np.pi / points)
    fourier = np.exp(-1j * angles) / np.sqrt(points)
    frequency = np.where(counter < points // 2, counter, counter - points) / points
    transfer = np.exp(-1j * FRESNEL * frequency * frequency)
    prop = (fourier * transfer[None, :]) @ fourier.conj()
    prop = 0.5 * (prop + prop.T)
    tables = []
    for matrix in (prop, fourier):
        re, im = matrix.real, matrix.imag
        right = np.block([[re, im], [-im, re]])
        left = np.block([[re, -im], [im, re]])
        tables.append(np.stack(split_table(right) + split_table(left)))
    return tables


def split(value):
    high = value.astype(BF16)
    low = (value - high.astype(F32)).astype(BF16)
    return high, low


def dot(a, b):
    return jnp.dot(a, b, preferred_element_type=F32)


def dot3(a, b):
    (a_high, a_low), (b_high, b_low) = a, b
    return dot(a_high, b_high) + (dot(a_high, b_low) + dot(a_low, b_high))


def apply_both(table_ref, fields, conj):
    n = fields[0].shape[0]
    first = 2 if conj else 0
    right = (table_ref[first], table_ref[first + 1])
    left = (table_ref[2 - first], table_ref[3 - first])
    mid = dot3(split(jnp.concatenate(fields, axis=0)), right)
    columns = [
        jnp.concatenate([mid[p * n : (p + 1) * n, :n], mid[p * n : (p + 1) * n, n:]], axis=0)
        for p in range(len(fields))
    ]
    out = dot3(left, split(jnp.concatenate(columns, axis=1)))
    return [
        jnp.concatenate([out[:n, p * n : (p + 1) * n], out[n:, p * n : (p + 1) * n]], axis=1)
        for p in range(len(fields))
    ]


def times(a, b):
    n = a.shape[-1] // 2
    ar, ai, br, bi = a[:, :n], a[:, n:], b[:, :n], b[:, n:]
    return jnp.concatenate([ar * br - ai * bi, ar * bi + ai * br], axis=1)


def conj_times(a, b):
    n = a.shape[-1] // 2
    ar, ai, br, bi = a[:, :n], a[:, n:], b[:, :n], b[:, n:]
    return jnp.concatenate([ar * br + ai * bi, ar * bi - ai * br], axis=1)


def groups_of(positions):
    size = 2 if positions % 2 == 0 else 1
    return [list(range(s, s + size)) for s in range(0, positions, size)]


def forward(prop_ref, factor_ref, incident_ref, wave_ref):
    positions, slabs = factor_ref.shape[:2]

    @pl.loop(0, slabs)
    def _(k):
        for group in groups_of(positions):
            waves = [wave_ref[p] for p in group]
            for p, wave in zip(group, waves):
                incident_ref[p, k] = wave
            waves = [times(wave, factor_ref[p, k]) for p, wave in zip(group, waves)]
            for p, wave in zip(group, apply_both(prop_ref, waves, False)):
                wave_ref[p] = wave


def backward(prop_ref, factor_ref, incident_ref, wave_ref, emit):
    positions, slabs = factor_ref.shape[:2]

    @pl.loop(0, slabs)
    def _(step):
        k = slabs - 1 - step
        for group in groups_of(positions):
            waves = apply_both(prop_ref, [wave_ref[p] for p in group], True)
            for p, wave in zip(group, waves):
                emit(p, k, conj_times(incident_ref[p, k], wave))
                wave_ref[p] = conj_times(factor_ref[p, k], wave)


def cut_kernel(off_ref, own_ref, left_ref, right_ref, up_ref, down_ref, ul_ref, ur_ref, dl_ref,
               dr_ref, factor_ref, ext):
    positions, slabs, n, _ = factor_ref.shape
    rows, cols = own_ref.shape[2:]
    b = n // 2
    for k in range(slabs):
        for part in range(2):
            ext[part, k, b : b + rows, n : n + cols] = own_ref[part, k]
            ext[part, k, :b, n : n + cols] = up_ref[part, k]
            ext[part, k, b + rows : n + rows, n : n + cols] = down_ref[part, k]
            for left, right, at, size in (
                (ul_ref, ur_ref, 0, b), (left_ref, right_ref, b, rows), (dl_ref, dr_ref, b + rows, b)
            ):
                x, y = left[k], right[k]
                if part == 0:
                    x = pltpu.roll(x, b, 1)
                else:
                    y = pltpu.roll(y, b, 1)
                ext[part, k, at : at + size, :n] = x
                ext[part, k, at : at + size, n + cols :] = y
    for p in range(positions):
        down = lax.rem(off_ref[p, 0] + b, 8)
        row = pl.multiple_of(off_ref[p, 0] + b - down, 8)
        col = off_ref[p, 1] + n
        block = jnp.minimum(col // n, (cols + n) // n - 1)
        start = pl.multiple_of(block * n, n)
        shift = lax.rem(4 * n - (col - start), 2 * n)
        for k in range(slabs):
            parts = []
            for part in range(2):
                wide = ext[part, k, pl.ds(row, n + 8), pl.ds(start, 2 * n)]
                wide = pltpu.roll(wide, shift, 1)[:, :n]
                parts.append(pltpu.roll(wide, lax.rem(n + 8 - down, n + 8), 0)[:n])
            factor_ref[p, k] = jnp.concatenate([1.0 + parts[0], parts[1]], axis=1)


def first_kernel(wave_in, factor_ref, prop_ref, wave_out, incident):
    wave_out[...] = wave_in[...]
    forward(prop_ref, factor_ref, incident, wave_out)


def middle_kernel(shift_ref, wave_in, factor_ref, patterns_ref, prop_ref, fourier_ref,
                  grad_exit, grad_start, incident, error_ref):
    positions, _, n, _ = factor_ref.shape
    grad_start[...] = wave_in[...]
    forward(prop_ref, factor_ref, incident, grad_start)
    error = jnp.zeros((8, n), F32)
    for group in groups_of(positions):
        fars = apply_both(fourier_ref, [grad_start[p] for p in group], False)
        grads = []
        for p, far in zip(group, fars):
            measured = patterns_ref[p]
            measured = pltpu.roll(measured, lax.rem(2 * n - shift_ref[p, 0], n), 0)
            measured = pltpu.roll(measured, lax.rem(2 * n - shift_ref[p, 1], n), 1)
            fr, fi = far[:, :n], far[:, n:]
            residual = fr * fr + fi * fi - measured
            error += jnp.sum((residual * residual).reshape(n // 8, 8, n), axis=0)
            residual = 2.0 * residual
            grads.append(jnp.concatenate([residual * fr, residual * fi], axis=1))
        for p, grad in zip(group, apply_both(fourier_ref, grads, True)):
            grad_exit[p] = grad
    error_ref[...] = error * 0.5
    grad_start[...] = grad_exit[...]
    backward(prop_ref, factor_ref, incident, grad_start, lambda p, k, piece: None)


def last_kernel(off_ref, wave_in, factor_ref, incident_ref, prop_ref, grad_start, center, up, down,
                left_ref, right_ref, ul_ref, ur_ref, dl_ref, dr_ref, ext):
    positions, slabs, n, _ = factor_ref.shape
    rows, cols = center.shape[2:]
    b = n // 2
    ext[...] = jnp.zeros_like(ext)
    grad_start[...] = wave_in[...]

    def emit(p, k, piece):
        down = lax.rem(off_ref[p, 0] + b, 8)
        row = pl.multiple_of(off_ref[p, 0] + b - down, 8)
        col = off_ref[p, 1] + n
        block = jnp.minimum(col // n, (cols + n) // n - 1)
        start = pl.multiple_of(block * n, n)
        shift = lax.rem(col - start, 2 * n)
        for part in range(2):
            value = piece[:, part * n : (part + 1) * n]
            value = jnp.concatenate([value, jnp.zeros((8, n), F32)], axis=0)
            value = pltpu.roll(value, down, 0)
            wide = pltpu.roll(jnp.concatenate([value, jnp.zeros_like(value)], axis=1), shift, 1)
            ext[part, k, pl.ds(row, n + 8), pl.ds(start, 2 * n)] += wide

    backward(prop_ref, factor_ref, incident_ref, grad_start, emit)
    lane = lax.broadcasted_iota(jnp.int32, (1, n), 1)
    for k in range(slabs):
        for part in range(2):
            center[part, k] = ext[part, k, b : b + rows, n : n + cols]
            up[part, k] = ext[part, k, :b, n : n + cols]
            down[part, k] = ext[part, k, b + rows : n + rows, n : n + cols]
        for left, right, at, size in (
            (ul_ref, ur_ref, 0, b), (left_ref, right_ref, b, rows), (dl_ref, dr_ref, b + rows, b)
        ):
            re, im = (ext[part, k, at : at + size, :n] for part in range(2))
            left[k] = jnp.where(lane < b, pltpu.roll(re, b, 1), im)
            re, im = (ext[part, k, at : at + size, n + cols :] for part in range(2))
            right[k] = jnp.where(lane < b, re, pltpu.roll(im, b, 1))


def fold_kernel(center, up, down, left_ref, right_ref, ul_ref, ur_ref, dl_ref, dr_ref, out):
    slabs, rows, cols = center.shape[1:]
    b = up.shape[2]
    n = 2 * b
    lane = lax.broadcasted_iota(jnp.int32, (1, n), 1)
    for k in range(slabs):
        for part in range(2):
            out[part, k] = center[part, k]
            out[part, k, :b] += up[part, k]
            out[part, k, rows - b :] += down[part, k]
            for left, right, at, size in (
                (left_ref, right_ref, 0, rows), (ul_ref, ur_ref, 0, b), (dl_ref, dr_ref, rows - b, b)
            ):
                x, y = left[k], right[k]
                if part == 1:
                    x = pltpu.roll(x, b, 1)
                else:
                    y = pltpu.roll(y, b, 1)
                out[part, k, at : at + size, :n] += jnp.where(lane < b, x, 0.0)
                out[part, k, at : at + size, cols - n :] += jnp.where(lane < b, 0.0, y)


VMEM = pl.BlockSpec(memory_space=pltpu.VMEM)
SMEM = pl.BlockSpec(memory_space=pltpu.SMEM)


def call(kernel, args, outs, smem=0, scratch=(), flops=0):
    return pl.pallas_call(
        kernel,
        out_shape=[jax.ShapeDtypeStruct(shape, F32) for shape in outs],
        in_specs=[SMEM] * smem + [VMEM] * (len(args) - smem),
        out_specs=[VMEM] * len(outs),
        scratch_shapes=[pltpu.VMEM(shape, F32) for shape in scratch],
        compiler_params=pltpu.CompilerParams(vmem_limit_bytes=48 * 1024 * 1024),
        cost_estimate=pl.CostEstimate(flops=flops, bytes_accessed=0, transcendentals=0),
    )(*args)


def shifted(value, down, right):
    rows, cols = lax.axis_size("sx"), lax.axis_size("sy")
    if right == 0:
        return lax.ppermute(value, "sx", [(i, i + down) for i in range(rows) if 0 <= i + down < rows])
    if down == 0:
        return lax.ppermute(value, "sy", [(i, i + right) for i in range(cols) if 0 <= i + right < cols])
    pairs = [
        (i * cols + j, (i + down) * cols + j + right)
        for i in range(rows)
        for j in range(cols)
        if 0 <= i + down < rows and 0 <= j + right < cols
    ]
    return lax.ppermute(value, ("sx", "sy"), pairs)


def local(probe_wave, transmission, scan_offsets, pattern_shifts, patterns):
    n = probe_wave.shape[-1]
    b = n // 2
    _, slabs, rows, cols = transmission.shape
    prop_table, fourier_table = (jnp.asarray(t) for t in build_tables(n))
    offsets = scan_offsets.reshape(-1, 2)
    shifts = pattern_shifts.reshape(-1, 2)
    measured = patterns.reshape(-1, n, n)
    positions = offsets.shape[0]
    depth = lax.axis_size("depth")
    index = lax.axis_index("depth")

    first = jnp.concatenate([transmission[0, :, :, :b], transmission[1, :, :, :b]], axis=-1)
    last = jnp.concatenate([transmission[0, :, :, cols - b :], transmission[1, :, :, cols - b :]], axis=-1)
    rims = [
        shifted(last, 0, 1),
        shifted(first, 0, -1),
        shifted(transmission[:, :, rows - b :], 1, 0),
        shifted(transmission[:, :, :b], -1, 0),
        shifted(last[:, rows - b :], 1, 1),
        shifted(first[:, rows - b :], 1, -1),
        shifted(last[:, :b], -1, 1),
        shifted(first[:, :b], -1, -1),
    ]
    wave_shape = (positions, n, 2 * n)
    store_shape = (positions, slabs, n, 2 * n)
    ext_shape = (2, slabs, rows + n + 8, cols + 2 * n)
    (factor,) = call(cut_kernel, [offsets, transmission, *rims], [store_shape], smem=1, scratch=[ext_shape])

    probe = jnp.broadcast_to(jnp.concatenate([probe_wave[0], probe_wave[1]], axis=-1)[None], wave_shape)
    forward_pairs = [(i, i + 1) for i in range(depth - 1)]
    backward_pairs = [(i + 1, i) for i in range(depth - 1)]
    entering = probe
    for _ in range(depth - 1):
        leaving, _ = call(first_kernel, [entering, factor, prop_table], [wave_shape, store_shape])
        incoming = lax.ppermute(leaving, "depth", forward_pairs)
        entering = jnp.where(index == 0, probe, incoming)
    grad_exit, grad_start, incident, error = call(
        middle_kernel, [shifts, entering, factor, measured, prop_table, fourier_table],
        [wave_shape, wave_shape, store_shape, (8, n)], smem=1,
    )
    for round_number in range(depth - 1):
        incoming = lax.ppermute(grad_start, "depth", backward_pairs)
        entering = jnp.where(index == depth - 1, grad_exit, incoming)
        grad_start, center, up, down, left, right, ul, ur, dl, dr = call(
            last_kernel, [offsets, entering, factor, incident, prop_table],
            [wave_shape, transmission.shape, (2, slabs, b, cols), (2, slabs, b, cols),
             (slabs, rows, n), (slabs, rows, n)] + [(slabs, b, n)] * 4,
            smem=1, scratch=[ext_shape],
        )
    probe_part = jnp.where(index == 0, jnp.sum(grad_start, axis=0), 0.0)
    error_part = jnp.where(index == depth - 1, error, 0.0)
    totals = lax.psum(jnp.concatenate([probe_part, jnp.concatenate([error_part, error_part * 0.0], axis=-1)], axis=0), ("sx", "sy", "depth"))
    (transmission_grad,) = call(
        fold_kernel,
        [center, shifted(down, 1, 0), shifted(up, -1, 0), shifted(right, 0, 1), shifted(left, 0, -1),
         shifted(dr, 1, 1), shifted(dl, 1, -1), shifted(ur, -1, 1), shifted(ul, -1, -1)],
        [transmission.shape],
    )
    all_positions = positions * lax.axis_size("sx") * lax.axis_size("sy")
    probe_grad = jnp.stack([totals[:n, :n], totals[:n, n:]]) / all_positions
    mean_error = jnp.sum(totals[n:]) / (all_positions * n * n)
    return (transmission_grad, probe_grad, mean_error)


def solution(mesh):
    in_specs = (
        P(),
        P(None, "depth", "sx", "sy"),
        P("sx", "sy", None, None),
        P("sx", "sy", None, None),
        P("sx", "sy", None, None, None),
    )
    out_specs = (P(None, "depth", "sx", "sy"), P(), P())
    return jax.shard_map(local, mesh=mesh, in_specs=in_specs, out_specs=out_specs, check_vma=False)
```

```python
import functools

import jax
import jax.numpy as jnp
import ml_dtypes
import numpy as np
from jax import lax
from jax.experimental import pallas as pl
from jax.experimental.pallas import tpu as pltpu
from jax.sharding import PartitionSpec as P

FRESNEL = 12.0
F32 = jnp.float32
BF16 = jnp.bfloat16


def split_table(table):
    high = table.astype(np.float32).astype(ml_dtypes.bfloat16)
    low = (table - high.astype(np.float64)).astype(np.float32).astype(ml_dtypes.bfloat16)
    return high, low


def build_tables(points):
    counter = np.arange(points)
    angles = (counter[:, None] * counter[None, :] % points) * (2.0 * np.pi / points)
    fourier = np.exp(-1j * angles) / np.sqrt(points)
    frequency = np.where(counter < points // 2, counter, counter - points) / points
    transfer = np.exp(-1j * FRESNEL * frequency * frequency)
    prop = (fourier * transfer[None, :]) @ fourier.conj()
    prop = 0.5 * (prop + prop.T)
    tables = []
    for matrix in (prop, fourier):
        re, im = matrix.real, matrix.imag
        right = np.block([[re, im], [-im, re]])
        left = np.block([[re, -im], [im, re]])
        tables.append(np.stack(split_table(right) + split_table(left)))
    return tables


def split(value):
    high = value.astype(BF16)
    low = (value - high.astype(F32)).astype(BF16)
    return high, low


def dot(a, b):
    return jnp.dot(a, b, preferred_element_type=F32)


def dot3(a, b):
    (a_high, a_low), (b_high, b_low) = a, b
    return dot(a_high, b_high) + (dot(a_high, b_low) + dot(a_low, b_high))


def apply_both(table_ref, fields, conj):
    n = fields[0].shape[0]
    first = 2 if conj else 0
    right = (table_ref[first], table_ref[first + 1])
    left = (table_ref[2 - first], table_ref[3 - first])
    mid = dot3(split(jnp.concatenate(fields, axis=0)), right)
    columns = [
        jnp.concatenate([mid[p * n : (p + 1) * n, :n], mid[p * n : (p + 1) * n, n:]], axis=0)
        for p in range(len(fields))
    ]
    out = dot3(left, split(jnp.concatenate(columns, axis=1)))
    return [
        jnp.concatenate([out[:n, p * n : (p + 1) * n], out[n:, p * n : (p + 1) * n]], axis=1)
        for p in range(len(fields))
    ]


def times(a, b):
    n = a.shape[-1] // 2
    ar, ai, br, bi = a[:, :n], a[:, n:], b[:, :n], b[:, n:]
    return jnp.concatenate([ar * br - ai * bi, ar * bi + ai * br], axis=1)


def conj_times(a, b):
    n = a.shape[-1] // 2
    ar, ai, br, bi = a[:, :n], a[:, n:], b[:, :n], b[:, n:]
    return jnp.concatenate([ar * br + ai * bi, ar * bi - ai * br], axis=1)


MESH = pl.DeviceIdType.MESH
SIDES = ((1, 0), (-1, 0), (0, 1), (0, -1), (1, 1), (1, -1), (-1, 1), (-1, -1))


def place():
    return tuple(lax.axis_index(name) for name in ("sx", "sy", "depth"))


def extent():
    return tuple(lax.axis_size(name) for name in ("sx", "sy", "depth"))


def inside(i, j, sizes):
    return (i >= 0) & (i < sizes[0]) & (j >= 0) & (j < sizes[1])


def greet(peers):
    barrier = pltpu.get_barrier_semaphore()
    for exists, device in peers:
        if exists is None:
            pl.semaphore_signal(barrier, inc=1, device_id=device, device_id_type=MESH)
        else:
            @pl.when(exists)
            def _():
                pl.semaphore_signal(barrier, inc=1, device_id=device, device_id_type=MESH)
    count = sum(jnp.int32(1) if exists is None else exists.astype(jnp.int32) for exists, _ in peers)
    pl.semaphore_wait(barrier, count)


def remote(source, target, send_sem, recv_sem, device):
    return pltpu.make_async_remote_copy(
        src_ref=source, dst_ref=target, send_sem=send_sem, recv_sem=recv_sem,
        device_id=device, device_id_type=MESH,
    )


class Rims:
    def __init__(self, sources, targets, send_sems, recv_sems):
        (i, j, d), sizes = place(), extent()
        self.items = []
        for at, (down, right) in enumerate(SIDES):
            copy = remote(sources[at], targets[at], send_sems.at[at], recv_sems.at[at],
                          (i + down, j + right, d))
            goes = inside(i + down, j + right, sizes)
            comes = inside(i - down, j - right, sizes)
            self.items.append((copy, goes, comes, targets[at]))

    def start(self, at):
        copy, goes, _, _ = self.items[at]
        pl.when(goes)(copy.start)

    def wait_recv(self, at):
        copy, _, comes, target = self.items[at]
        pl.when(comes)(copy.wait_recv)

        @pl.when(jnp.logical_not(comes))
        def _():
            target[...] = jnp.zeros_like(target)

    def wait_send(self, at):
        copy, goes, _, _ = self.items[at]
        pl.when(goes)(copy.wait_send)


def window_place(off_ref, p, n, cols):
    row = off_ref[p, 0] + n // 2
    down = lax.rem(row, 8)
    row = pl.multiple_of(row - down, 8)
    col = off_ref[p, 1] + n
    block = jnp.minimum(col // n, (cols + n) // n - 1)
    start = pl.multiple_of(block * n, n)
    return row, down, start, col - start


def rim_rows(b, rows):
    return ((0, b), (b, rows), (b + rows, b))


def halo_kernel(own_ref, *refs):
    outs, (first, last, *bufs), (send_sems, recv_sems) = refs[:8], refs[8:18], refs[18:]
    (i, j, d), sizes = place(), extent()
    slabs, rows, cols = own_ref.shape[1:]
    n = first.shape[-1]
    b = n // 2
    lane = lax.broadcasted_iota(jnp.int32, (1, n), 1)
    for k in range(slabs):
        re, im = (own_ref[part, k, :, :n] for part in range(2))
        first[k] = jnp.where(lane < b, re, pltpu.roll(im, b, 1))
        re, im = (own_ref[part, k, :, cols - n :] for part in range(2))
        last[k] = jnp.where(lane < b, pltpu.roll(re, b, 1), im)
    greet([(inside(i + y, j + x, sizes), (i + y, j + x, d)) for y, x in SIDES])
    low, high = pl.ds(rows - b, b), pl.ds(0, b)
    rims = Rims(
        [own_ref.at[:, :, low], own_ref.at[:, :, high], last, first,
         last.at[:, low], first.at[:, low], last.at[:, high], first.at[:, high]],
        bufs, send_sems, recv_sems,
    )
    for at in range(len(SIDES)):
        rims.start(at)
    for at in range(len(SIDES)):
        rims.wait_recv(at)
        outs[at][...] = bufs[at][...]
    for at in range(len(SIDES)):
        rims.wait_send(at)


def cut_kernel(off_ref, shift_ref, own_ref, patterns_ref, up, down, left, right, ul, ur, dl, dr,
               factor, measured, ext):
    positions, slabs, n, _ = factor.shape
    rows, cols = own_ref.shape[2:]
    b = n // 2
    for k in range(slabs):
        for part in range(2):
            ext[part, k, b : b + rows, n : n + cols] = own_ref[part, k]
            ext[part, k, :b, n : n + cols] = up[part, k]
            ext[part, k, b + rows : n + rows, n : n + cols] = down[part, k]
            for (x_ref, y_ref), (at, size) in zip(((ul, ur), (left, right), (dl, dr)), rim_rows(b, rows)):
                x, y = x_ref[k], y_ref[k]
                if part == 0:
                    x = pltpu.roll(x, b, 1)
                else:
                    y = pltpu.roll(y, b, 1)
                ext[part, k, at : at + size, :n] = x
                ext[part, k, at : at + size, n + cols :] = y
    for p in range(positions):
        value = pltpu.roll(patterns_ref[p], lax.rem(2 * n - shift_ref[p, 0], n), 0)
        measured[p] = pltpu.roll(value, lax.rem(2 * n - shift_ref[p, 1], n), 1)
        row, off, start, shift = window_place(off_ref, p, n, cols)
        for k in range(slabs):
            parts = []
            for part in range(2):
                wide = ext[part, k, pl.ds(row, n + 8), pl.ds(start, 2 * n)]
                wide = pltpu.roll(wide, lax.rem(2 * n - shift, 2 * n), 1)[:, :n]
                parts.append(pltpu.roll(wide, lax.rem(n + 8 - off, n + 8), 0)[:n])
            factor[p, k] = jnp.concatenate([1.0 + parts[0], parts[1]], axis=1)


def wave_kernel(group_size, factor, probe_ref, measured, prop_ref, fourier_ref, piece_ref, red_ref,
                incident, wave, arrived, grad, returned, error, error_in,
                wave_send, wave_recv, grad_send, grad_recv, error_send, error_recv):
    (i, j, d), sizes = place(), extent()
    depth = sizes[2]
    positions, slabs, n, _ = factor.shape
    final = depth - 1
    greet([(None, (i, j, lax.rem(d + step, depth))) for step in range(1, depth)])
    error[...] = jnp.zeros_like(error)

    def wave_copy(p):
        return remote(wave.at[p], arrived.at[p], wave_send.at[p], wave_recv.at[p], (i, j, d + 1))

    def grad_copy(p):
        return remote(grad.at[p], returned.at[p], grad_send.at[p], grad_recv.at[p], (i, j, d - 1))

    error_copy = remote(error, error_in, error_send, error_recv, (i, j, 0))

    def backward(group):
        @pl.loop(0, slabs)
        def _(step):
            k = slabs - 1 - step
            for p, value in zip(group, apply_both(prop_ref, [grad[p] for p in group], True)):
                piece_ref[p, k] = conj_times(incident[p, k], value)
                grad[p] = conj_times(factor[p, k], value)

    groups = [list(range(g, g + group_size)) for g in range(0, positions, group_size)]

    for group in groups:
        @pl.when(d == 0)
        def _():
            for p in group:
                wave[p] = probe_ref[...]

        @pl.when(d > 0)
        def _():
            for p in group:
                wave_copy(p).wait_recv()
                wave[p] = arrived[p]

        @pl.loop(0, slabs)
        def _(k):
            values = [wave[p] for p in group]
            for p, value in zip(group, values):
                incident[p, k] = value
            values = [times(value, factor[p, k]) for p, value in zip(group, values)]
            for p, value in zip(group, apply_both(prop_ref, values, False)):
                wave[p] = value

        @pl.when(d < final)
        def _():
            for p in group:
                wave_copy(p).start()

        @pl.when(d == final)
        def _():
            fars = apply_both(fourier_ref, [wave[p] for p in group], False)
            values = []
            for p, far in zip(group, fars):
                fr, fi = far[:, :n], far[:, n:]
                residual = fr * fr + fi * fi - measured[p]
                error[:, :n] += jnp.sum((residual * residual).reshape(n // 8, 8, n), axis=0)
                residual = 2.0 * residual
                values.append(jnp.concatenate([residual * fr, residual * fi], axis=1))
            for p, value in zip(group, apply_both(fourier_ref, values, True)):
                grad[p] = value
            backward(group)
            for p in group:
                grad_copy(p).start()

    @pl.when(d == final)
    def _():
        error_copy.start()

    @pl.when(d < final)
    def _():
        for group in groups:
            for p in group:
                grad_copy_in(p, grad, returned, grad_send, grad_recv, (i, j, d + 1)).wait_recv()
                grad[p] = returned[p]
            backward(group)

            @pl.when(d > 0)
            def _():
                for p in group:
                    grad_copy(p).start()

    @pl.when(d == 0)
    def _():
        error_copy_in = remote(error, error_in, error_send, error_recv, (i, j, final))
        error_copy_in.wait_recv()
        total = grad[0]
        for p in range(1, positions):
            total = total + grad[p]
        height = n // red_ref.shape[0]
        for part in range(red_ref.shape[0]):
            red_ref[part, :height] = total[part * height : (part + 1) * height]
            red_ref[part, height:] = error_in[...]

    @pl.when(d > 0)
    def _():
        red_ref[...] = jnp.zeros_like(red_ref)
        for p in range(positions):
            grad_copy(p).wait_send()

    @pl.when(d == final)
    def _():
        error_copy.wait_send()

    @pl.when(d < final)
    def _():
        for p in range(positions):
            wave_copy(p).wait_send()


def grad_copy_in(p, grad, returned, grad_send, grad_recv, device):
    return remote(grad.at[p], returned.at[p], grad_send.at[p], grad_recv.at[p], device)


def scatter_kernel(off_ref, piece_ref, center, up, down, left_ref, right_ref, ul_ref, ur_ref, dl_ref,
                   dr_ref, ext):
    positions, slabs, n, _ = piece_ref.shape
    rows, cols = center.shape[2:]
    b = n // 2
    ext[...] = jnp.zeros_like(ext)
    for p in range(positions):
        row, off, start, shift = window_place(off_ref, p, n, cols)
        for k in range(slabs):
            for part in range(2):
                value = piece_ref[p, k, :, part * n : (part + 1) * n]
                value = jnp.concatenate([value, jnp.zeros((8, n), F32)], axis=0)
                value = pltpu.roll(value, off, 0)
                wide = jnp.concatenate([value, jnp.zeros_like(value)], axis=1)
                ext[part, k, pl.ds(row, n + 8), pl.ds(start, 2 * n)] += pltpu.roll(wide, lax.rem(shift, 2 * n), 1)
    lane = lax.broadcasted_iota(jnp.int32, (1, n), 1)
    for k in range(slabs):
        for part in range(2):
            center[part, k] = ext[part, k, b : b + rows, n : n + cols]
            up[part, k] = ext[part, k, :b, n : n + cols]
            down[part, k] = ext[part, k, b + rows : n + rows, n : n + cols]
        for left, right, (at, size) in zip(
            (ul_ref, left_ref, dl_ref), (ur_ref, right_ref, dr_ref), rim_rows(b, rows)
        ):
            re, im = (ext[part, k, at : at + size, :n] for part in range(2))
            left[k] = jnp.where(lane < b, pltpu.roll(re, b, 1), im)
            re, im = (ext[part, k, at : at + size, n + cols :] for part in range(2))
            right[k] = jnp.where(lane < b, re, pltpu.roll(im, b, 1))


def fold_kernel(center, to_up, to_down, to_left, to_right, to_ul, to_ur, to_dl, to_dr, red_ref,
                out, total_ref, up, down, left, right, ul, ur, dl, dr, part_in, column_in, mine,
                whole, send_sems, recv_sems, part_send, part_recv, column_send, column_recv,
                whole_send, whole_recv):
    (i, j, d), sizes = place(), extent()
    n_sx, n_sy, depth = sizes
    slabs, rows, cols = center.shape[1:]
    b = up.shape[2]
    n = 2 * b
    across = [lax.rem(i + step, n_sx) for step in range(1, n_sx)]
    along = [lax.rem(j + step, n_sy) for step in range(1, n_sy)]
    peers = [(None, (x, j, d)) for x in across] + [(None, (i, y, d)) for y in along]
    peers += [(inside(i + y, j + x, sizes), (i + y, j + x, d)) for y, x in SIDES if y and x]
    others = [(x, lax.rem(d + step, depth)) for step in range(1, depth) for x in range(n_sx)]
    peers += [(None, (x, j, z)) for x, z in others]
    greet(peers)
    rims = Rims([to_down, to_up, to_right, to_left, to_dr, to_dl, to_ur, to_ul],
                [up, down, left, right, ul, ur, dl, dr], send_sems, recv_sems)

    parts = [
        remote(red_ref.at[x], part_in.at[step], part_send.at[step], part_recv.at[step], (x, j, d))
        for step, x in enumerate(across)
    ]
    columns = [
        remote(mine, column_in.at[j], column_send.at[step], column_recv.at[j], (i, y, d))
        for step, y in enumerate(along)
    ]
    wholes = [
        remote(whole.at[i], whole.at[i], whole_send.at[step], whole_recv.at[i], (x, j, z))
        for step, (x, z) in enumerate([(x, d) for x in across] + others)
    ]

    @pl.when(d == 0)
    def _():
        for copy in parts:
            copy.start()

    rims.start(0)
    rims.start(1)

    @pl.when(d == 0)
    def _():
        value = red_ref[i]
        for step, copy in enumerate(parts):
            copy.wait_recv()
            value = value + part_in[step]
        mine[...] = value
        for copy in columns:
            copy.start()

    for at in range(2, len(SIDES)):
        rims.start(at)
    for k in range(slabs):
        for part in range(2):
            out[part, k] = center[part, k]

    @pl.when(d == 0)
    def _():
        for step in range(1, n_sy):
            y = lax.rem(j + n_sy - step, n_sy)
            remote(mine, column_in.at[y], column_send.at[step - 1], column_recv.at[y], (i, y, d)).wait_recv()
        column_in[j] = mine[...]
        value = column_in[0]
        for y in range(1, n_sy):
            value = value + column_in[y]
        whole[i] = value
        for copy in wholes:
            copy.start()

    for at in range(2):
        rims.wait_recv(at)
    for k in range(slabs):
        for part in range(2):
            out[part, k, :b] += up[part, k]
            out[part, k, rows - b :] += down[part, k]
    for at in range(2, len(SIDES)):
        rims.wait_recv(at)
    lane = lax.broadcasted_iota(jnp.int32, (1, n), 1)
    for k in range(slabs):
        for part in range(2):
            for x_ref, y_ref, at, size in ((left, right, 0, rows), (ul, ur, 0, b), (dl, dr, rows - b, b)):
                x, y = x_ref[k], y_ref[k]
                if part == 1:
                    x = pltpu.roll(x, b, 1)
                else:
                    y = pltpu.roll(y, b, 1)
                out[part, k, at : at + size, :n] += jnp.where(lane < b, x, 0.0)
                out[part, k, at : at + size, cols - n :] += jnp.where(lane < b, 0.0, y)

    def whole_arrives(x):
        remote(whole.at[x], whole.at[x], whole_send.at[0], whole_recv.at[x], (x, j, d)).wait_recv()

    for x in across:
        whole_arrives(x)
    pl.when(d > 0)(lambda: whole_arrives(i))
    for x in range(n_sx):
        total_ref[x] = whole[x]

    @pl.when(d == 0)
    def _():
        for copy in parts + columns + wholes:
            copy.wait_send()

    for at in range(len(SIDES)):
        rims.wait_send(at)


VMEM = pl.BlockSpec(memory_space=pltpu.VMEM)
SMEM = pl.BlockSpec(memory_space=pltpu.SMEM)


def call(kernel, args, outs, smem=0, scratch=(), sems=(), collective=None):
    params = dict(vmem_limit_bytes=48 * 1024 * 1024)
    if collective is not None:
        params.update(collective_id=collective, has_side_effects=True)
    return pl.pallas_call(
        kernel,
        out_shape=[jax.ShapeDtypeStruct(shape, F32) for shape in outs],
        in_specs=[SMEM] * smem + [VMEM] * (len(args) - smem),
        out_specs=[VMEM] * len(outs),
        scratch_shapes=[pltpu.VMEM(shape, F32) for shape in scratch]
        + [pltpu.SemaphoreType.DMA(shape) if shape else pltpu.SemaphoreType.DMA for shape in sems],
        compiler_params=pltpu.CompilerParams(**params),
    )(*args)


def local(probe_wave, transmission, scan_offsets, pattern_shifts, patterns):
    n = probe_wave.shape[-1]
    b = n // 2
    _, slabs, rows, cols = transmission.shape
    prop_table, fourier_table = (jnp.asarray(t) for t in build_tables(n))
    offsets = scan_offsets.reshape(-1, 2)
    shifts = pattern_shifts.reshape(-1, 2)
    measured = patterns.reshape(-1, n, n)
    positions = offsets.shape[0]
    n_sx, n_sy, depth = extent()
    probe = jnp.concatenate([probe_wave[0], probe_wave[1]], axis=-1)

    wave_shape = (positions, n, 2 * n)
    store_shape = (positions, slabs, n, 2 * n)
    ext_shape = (2, slabs, rows + n + 8, cols + 2 * n)
    side_shape, edge_shape, corner_shape = (slabs, rows, n), (2, slabs, b, cols), (slabs, b, n)
    rim_shapes = [edge_shape] * 2 + [side_shape] * 2 + [corner_shape] * 4
    chunk = (n // n_sx + 8, 2 * n)
    sides = (len(SIDES),)
    rims = call(halo_kernel, [transmission], rim_shapes, scratch=[side_shape] * 2 + rim_shapes,
                sems=[sides] * 2, collective=0)
    factor, moved = call(
        cut_kernel, [offsets, shifts, transmission, measured, *rims],
        [store_shape, (positions, n, n)], smem=2, scratch=[ext_shape],
    )
    pieces, red = call(
        functools.partial(wave_kernel, 2 if positions % 2 == 0 else 1),
        [factor, probe, moved, prop_table, fourier_table], [store_shape, (n_sx, *chunk)],
        scratch=[store_shape] + [wave_shape] * 4 + [(8, 2 * n)] * 2,
        sems=[(positions,)] * 4 + [()] * 2, collective=2,
    )
    rims = call(scatter_kernel, [offsets, pieces], [transmission.shape, *rim_shapes], smem=1, scratch=[ext_shape])
    transmission_grad, totals = call(
        fold_kernel, [*rims, red], [transmission.shape, (n_sx, *chunk)],
        scratch=rim_shapes + [(n_sx - 1, *chunk), (n_sy, *chunk), chunk, (n_sx, *chunk)],
        sems=[sides] * 2 + [(n_sx - 1,)] * 2 + [(n_sy - 1,), (n_sy,), (n_sx * depth - 1,), (n_sx,)], collective=1,
    )
    all_positions = positions * n_sx * n_sy
    summed = totals[:, : n // n_sx].reshape(n, 2 * n)
    probe_grad = jnp.stack([summed[:, :n], summed[:, n:]]) / all_positions
    mean_error = 0.5 * jnp.sum(totals[0, n // n_sx :, :n]) / (all_positions * n * n)
    return (transmission_grad, probe_grad, mean_error)


def solution(mesh):
    in_specs = (
        P(),
        P(None, "depth", "sx", "sy"),
        P("sx", "sy", None, None),
        P("sx", "sy", None, None),
        P("sx", "sy", None, None, None),
    )
    out_specs = (P(None, "depth", "sx", "sy"), P(), P())
    return jax.shard_map(local, mesh=mesh, in_specs=in_specs, out_specs=out_specs, check_vma=False)
```

```python
import functools

import jax
import jax.numpy as jnp
import ml_dtypes
import numpy as np
from jax import lax
from jax.experimental import pallas as pl
from jax.experimental.pallas import tpu as pltpu
from jax.sharding import PartitionSpec as P

FRESNEL = 12.0
F32 = jnp.float32
BF16 = jnp.bfloat16


def split_table(table):
    high = table.astype(np.float32).astype(ml_dtypes.bfloat16)
    low = (table - high.astype(np.float64)).astype(np.float32).astype(ml_dtypes.bfloat16)
    return high, low


def build_tables(points):
    counter = np.arange(points)
    angles = (counter[:, None] * counter[None, :] % points) * (2.0 * np.pi / points)
    fourier = np.exp(-1j * angles) / np.sqrt(points)
    frequency = np.where(counter < points // 2, counter, counter - points) / points
    transfer = np.exp(-1j * FRESNEL * frequency * frequency)
    prop = (fourier * transfer[None, :]) @ fourier.conj()
    prop = 0.5 * (prop + prop.T)
    tables = []
    for matrix in (prop, fourier):
        re, im = matrix.real, matrix.imag
        right = np.block([[re, im], [-im, re]])
        left = np.block([[re, -im], [im, re]])
        tables.append(np.stack(split_table(right) + split_table(left)))
    return tables


def split(value):
    high = value.astype(BF16)
    low = (value - high.astype(F32)).astype(BF16)
    return high, low


def dot(a, b):
    return jnp.dot(a, b, preferred_element_type=F32)


def dot3(a, b):
    (a_high, a_low), (b_high, b_low) = a, b
    return dot(a_high, b_high) + (dot(a_high, b_low) + dot(a_low, b_high))


def apply_both(table_ref, fields, conj):
    n = fields[0].shape[0]
    first = 2 if conj else 0
    right = (table_ref[first], table_ref[first + 1])
    left = (table_ref[2 - first], table_ref[3 - first])
    mid = dot3(split(jnp.concatenate(fields, axis=0)), right)
    columns = [
        jnp.concatenate([mid[p * n : (p + 1) * n, :n], mid[p * n : (p + 1) * n, n:]], axis=0)
        for p in range(len(fields))
    ]
    out = dot3(left, split(jnp.concatenate(columns, axis=1)))
    return [
        jnp.concatenate([out[:n, p * n : (p + 1) * n], out[n:, p * n : (p + 1) * n]], axis=1)
        for p in range(len(fields))
    ]


def times(a, b):
    n = a.shape[-1] // 2
    ar, ai, br, bi = a[:, :n], a[:, n:], b[:, :n], b[:, n:]
    return jnp.concatenate([ar * br - ai * bi, ar * bi + ai * br], axis=1)


def conj_times(a, b):
    n = a.shape[-1] // 2
    ar, ai, br, bi = a[:, :n], a[:, n:], b[:, :n], b[:, n:]
    return jnp.concatenate([ar * br + ai * bi, ar * bi - ai * br], axis=1)


MESH = pl.DeviceIdType.MESH
SIDES = ((1, 0), (-1, 0), (0, 1), (0, -1), (1, 1), (1, -1), (-1, 1), (-1, -1))


def place():
    return tuple(lax.axis_index(name) for name in ("sx", "sy", "depth"))


def extent():
    return tuple(lax.axis_size(name) for name in ("sx", "sy", "depth"))


def inside(i, j, sizes):
    return (i >= 0) & (i < sizes[0]) & (j >= 0) & (j < sizes[1])


def greet(peers):
    barrier = pltpu.get_barrier_semaphore()
    for exists, device in peers:
        if exists is None:
            pl.semaphore_signal(barrier, inc=1, device_id=device, device_id_type=MESH)
        else:
            @pl.when(exists)
            def _():
                pl.semaphore_signal(barrier, inc=1, device_id=device, device_id_type=MESH)
    count = sum(jnp.int32(1) if exists is None else exists.astype(jnp.int32) for exists, _ in peers)
    pl.semaphore_wait(barrier, count)


def remote(source, target, send_sem, recv_sem, device):
    return pltpu.make_async_remote_copy(
        src_ref=source, dst_ref=target, send_sem=send_sem, recv_sem=recv_sem,
        device_id=device, device_id_type=MESH,
    )


class Rims:
    def __init__(self, sources, targets, send_sems, recv_sems):
        (i, j, d), sizes = place(), extent()
        self.items = []
        for at, (down, right) in enumerate(SIDES):
            copy = remote(sources[at], targets[at], send_sems.at[at], recv_sems.at[at],
                          (i + down, j + right, d))
            goes = inside(i + down, j + right, sizes)
            comes = inside(i - down, j - right, sizes)
            self.items.append((copy, goes, comes, targets[at]))

    def start(self, at):
        copy, goes, _, _ = self.items[at]
        pl.when(goes)(copy.start)

    def wait_recv(self, at):
        copy, _, comes, target = self.items[at]
        pl.when(comes)(copy.wait_recv)

        @pl.when(jnp.logical_not(comes))
        def _():
            target[...] = jnp.zeros_like(target)

    def wait_send(self, at):
        copy, goes, _, _ = self.items[at]
        pl.when(goes)(copy.wait_send)


def window_place(off_ref, p, n, cols):
    row = off_ref[p, 0] + n // 2
    down = lax.rem(row, 8)
    row = pl.multiple_of(row - down, 8)
    col = off_ref[p, 1] + n
    block = jnp.minimum(col // n, (cols + n) // n - 1)
    start = pl.multiple_of(block * n, n)
    return row, down, start, col - start


def rim_rows(b, rows):
    return ((0, b), (b, rows), (b + rows, b))


def halo_kernel(own_ref, *refs):
    outs, (first, last, *bufs), (send_sems, recv_sems) = refs[:8], refs[8:18], refs[18:]
    (i, j, d), sizes = place(), extent()
    slabs, rows, cols = own_ref.shape[1:]
    n = first.shape[-1]
    b = n // 2
    lane = lax.broadcasted_iota(jnp.int32, (1, n), 1)
    for k in range(slabs):
        re, im = (own_ref[part, k, :, :n] for part in range(2))
        first[k] = jnp.where(lane < b, re, pltpu.roll(im, b, 1))
        re, im = (own_ref[part, k, :, cols - n :] for part in range(2))
        last[k] = jnp.where(lane < b, pltpu.roll(re, b, 1), im)
    greet([(inside(i + y, j + x, sizes), (i + y, j + x, d)) for y, x in SIDES])
    low, high = pl.ds(rows - b, b), pl.ds(0, b)
    rims = Rims(
        [own_ref.at[:, :, low], own_ref.at[:, :, high], last, first,
         last.at[:, low], first.at[:, low], last.at[:, high], first.at[:, high]],
        bufs, send_sems, recv_sems,
    )
    for at in range(len(SIDES)):
        rims.start(at)
    for at in range(len(SIDES)):
        rims.wait_recv(at)
        outs[at][...] = bufs[at][...]
    for at in range(len(SIDES)):
        rims.wait_send(at)


def cut_kernel(off_ref, shift_ref, own_ref, patterns_ref, up, down, left, right, ul, ur, dl, dr,
               factor, measured, ext):
    positions, slabs, n, _ = factor.shape
    rows, cols = own_ref.shape[2:]
    b = n // 2
    for k in range(slabs):
        for part in range(2):
            ext[part, k, b : b + rows, n : n + cols] = own_ref[part, k]
            ext[part, k, :b, n : n + cols] = up[part, k]
            ext[part, k, b + rows : n + rows, n : n + cols] = down[part, k]
            for (x_ref, y_ref), (at, size) in zip(((ul, ur), (left, right), (dl, dr)), rim_rows(b, rows)):
                x, y = x_ref[k], y_ref[k]
                if part == 0:
                    x = pltpu.roll(x, b, 1)
                else:
                    y = pltpu.roll(y, b, 1)
                ext[part, k, at : at + size, :n] = x
                ext[part, k, at : at + size, n + cols :] = y
    for p in range(positions):
        value = pltpu.roll(patterns_ref[p], lax.rem(2 * n - shift_ref[p, 0], n), 0)
        measured[p] = pltpu.roll(value, lax.rem(2 * n - shift_ref[p, 1], n), 1)
        row, off, start, shift = window_place(off_ref, p, n, cols)
        for k in range(slabs):
            parts = []
            for part in range(2):
                wide = ext[part, k, pl.ds(row, n + 8), pl.ds(start, 2 * n)]
                wide = pltpu.roll(wide, lax.rem(2 * n - shift, 2 * n), 1)[:, :n]
                parts.append(pltpu.roll(wide, lax.rem(n + 8 - off, n + 8), 0)[:n])
            factor[p, k] = jnp.concatenate([1.0 + parts[0], parts[1]], axis=1)


def wave_kernel(group_size, factor, probe_ref, measured, prop_ref, fourier_ref, piece_ref, red_ref,
                incident, wave, arrived, grad, returned, error, error_in,
                wave_send, wave_recv, grad_send, grad_recv, error_send, error_recv):
    (i, j, d), sizes = place(), extent()
    depth = sizes[2]
    positions, slabs, n, _ = factor.shape
    final = depth - 1
    greet([(None, (i, j, lax.rem(d + step, depth))) for step in range(1, depth)])
    error[...] = jnp.zeros_like(error)

    def wave_copy(p):
        return remote(wave.at[p], arrived.at[p], wave_send.at[p], wave_recv.at[p], (i, j, d + 1))

    def grad_copy(p):
        return remote(grad.at[p], returned.at[p], grad_send.at[p], grad_recv.at[p], (i, j, d - 1))

    error_copy = remote(error, error_in, error_send, error_recv, (i, j, 0))

    def backward(group):
        @pl.loop(0, slabs)
        def _(step):
            k = slabs - 1 - step
            for p, value in zip(group, apply_both(prop_ref, [grad[p] for p in group], True)):
                piece_ref[p, k] = conj_times(incident[p, k], value)
                grad[p] = conj_times(factor[p, k], value)

    groups = [list(range(g, g + group_size)) for g in range(0, positions, group_size)]

    for group in groups:
        @pl.when(d == 0)
        def _():
            for p in group:
                wave[p] = probe_ref[...]

        @pl.when(d > 0)
        def _():
            for p in group:
                wave_copy(p).wait_recv()
                wave[p] = arrived[p]

        @pl.loop(0, slabs)
        def _(k):
            values = [wave[p] for p in group]
            for p, value in zip(group, values):
                incident[p, k] = value
            values = [times(value, factor[p, k]) for p, value in zip(group, values)]
            for p, value in zip(group, apply_both(prop_ref, values, False)):
                wave[p] = value

        @pl.when(d < final)
        def _():
            for p in group:
                wave_copy(p).start()

        @pl.when(d == final)
        def _():
            fars = apply_both(fourier_ref, [wave[p] for p in group], False)
            values = []
            for p, far in zip(group, fars):
                fr, fi = far[:, :n], far[:, n:]
                residual = fr * fr + fi * fi - measured[p]
                error[:, :n] += jnp.sum((residual * residual).reshape(n // 8, 8, n), axis=0)
                residual = 2.0 * residual
                values.append(jnp.concatenate([residual * fr, residual * fi], axis=1))
            for p, value in zip(group, apply_both(fourier_ref, values, True)):
                grad[p] = value
            backward(group)
            for p in group:
                grad_copy(p).start()

    @pl.when(d == final)
    def _():
        error_copy.start()

    @pl.when(d < final)
    def _():
        for group in groups:
            for p in group:
                grad_copy_in(p, grad, returned, grad_send, grad_recv, (i, j, d + 1)).wait_recv()
                grad[p] = returned[p]
            backward(group)

            @pl.when(d > 0)
            def _():
                for p in group:
                    grad_copy(p).start()

    @pl.when(d == 0)
    def _():
        error_copy_in = remote(error, error_in, error_send, error_recv, (i, j, final))
        error_copy_in.wait_recv()
        total = grad[0]
        for p in range(1, positions):
            total = total + grad[p]
        height = n // red_ref.shape[0]
        for part in range(red_ref.shape[0]):
            red_ref[part, :height] = total[part * height : (part + 1) * height]
            red_ref[part, height:] = error_in[...]

    @pl.when(d > 0)
    def _():
        red_ref[...] = jnp.zeros_like(red_ref)
        for p in range(positions):
            grad_copy(p).wait_send()

    @pl.when(d == final)
    def _():
        error_copy.wait_send()

    @pl.when(d < final)
    def _():
        for p in range(positions):
            wave_copy(p).wait_send()


def grad_copy_in(p, grad, returned, grad_send, grad_recv, device):
    return remote(grad.at[p], returned.at[p], grad_send.at[p], grad_recv.at[p], device)


def scatter_kernel(off_ref, piece_ref, center, up, down, left_ref, right_ref, ul_ref, ur_ref, dl_ref,
                   dr_ref, ext):
    positions, slabs, n, _ = piece_ref.shape
    rows, cols = center.shape[2:]
    b = n // 2
    ext[...] = jnp.zeros_like(ext)
    for p in range(positions):
        row, off, start, shift = window_place(off_ref, p, n, cols)
        for k in range(slabs):
            for part in range(2):
                value = piece_ref[p, k, :, part * n : (part + 1) * n]
                value = jnp.concatenate([value, jnp.zeros((8, n), F32)], axis=0)
                value = pltpu.roll(value, off, 0)
                wide = jnp.concatenate([value, jnp.zeros_like(value)], axis=1)
                ext[part, k, pl.ds(row, n + 8), pl.ds(start, 2 * n)] += pltpu.roll(wide, lax.rem(shift, 2 * n), 1)
    lane = lax.broadcasted_iota(jnp.int32, (1, n), 1)
    for k in range(slabs):
        for part in range(2):
            center[part, k] = ext[part, k, b : b + rows, n : n + cols]
            up[part, k] = ext[part, k, :b, n : n + cols]
            down[part, k] = ext[part, k, b + rows : n + rows, n : n + cols]
        for left, right, (at, size) in zip(
            (ul_ref, left_ref, dl_ref), (ur_ref, right_ref, dr_ref), rim_rows(b, rows)
        ):
            re, im = (ext[part, k, at : at + size, :n] for part in range(2))
            left[k] = jnp.where(lane < b, pltpu.roll(re, b, 1), im)
            re, im = (ext[part, k, at : at + size, n + cols :] for part in range(2))
            right[k] = jnp.where(lane < b, re, pltpu.roll(im, b, 1))


def fold_kernel(center, to_up, to_down, to_left, to_right, to_ul, to_ur, to_dl, to_dr, red_ref,
                out, total_ref, up, down, left, right, ul, ur, dl, dr, part_in, column_in, mine,
                whole, send_sems, recv_sems, part_send, part_recv, column_send, column_recv,
                whole_send, whole_recv):
    (i, j, d), sizes = place(), extent()
    n_sx, n_sy, depth = sizes
    slabs, rows, cols = center.shape[1:]
    b = up.shape[2]
    n = 2 * b
    across = [lax.rem(i + step, n_sx) for step in range(1, n_sx)]
    along = [lax.rem(j + step, n_sy) for step in range(1, n_sy)]
    peers = [(None, (x, j, d)) for x in across] + [(None, (i, y, d)) for y in along]
    peers += [(inside(i + y, j + x, sizes), (i + y, j + x, d)) for y, x in SIDES if y and x]
    others = [(x, lax.rem(d + step, depth)) for step in range(1, depth) for x in range(n_sx)]
    peers += [(None, (x, j, z)) for x, z in others]
    greet(peers)
    rims = Rims([to_down, to_up, to_right, to_left, to_dr, to_dl, to_ur, to_ul],
                [up, down, left, right, ul, ur, dl, dr], send_sems, recv_sems)

    parts = [
        remote(red_ref.at[x], part_in.at[step], part_send.at[step], part_recv.at[step], (x, j, d))
        for step, x in enumerate(across)
    ]
    columns = [
        remote(mine, column_in.at[j], column_send.at[step], column_recv.at[j], (i, y, d))
        for step, y in enumerate(along)
    ]
    wholes = [
        remote(whole.at[i], whole.at[i], whole_send.at[step], whole_recv.at[i], (x, j, z))
        for step, (x, z) in enumerate([(x, d) for x in across] + others)
    ]

    @pl.when(d == 0)
    def _():
        for copy in parts:
            copy.start()

    rims.start(0)
    rims.start(1)

    @pl.when(d == 0)
    def _():
        value = red_ref[i]
        for step, copy in enumerate(parts):
            copy.wait_recv()
            value = value + part_in[step]
        mine[...] = value
        for copy in columns:
            copy.start()

    for at in range(2, len(SIDES)):
        rims.start(at)
    for k in range(slabs):
        for part in range(2):
            out[part, k] = center[part, k]

    @pl.when(d == 0)
    def _():
        for step in range(1, n_sy):
            y = lax.rem(j + n_sy - step, n_sy)
            remote(mine, column_in.at[y], column_send.at[step - 1], column_recv.at[y], (i, y, d)).wait_recv()
        column_in[j] = mine[...]
        value = column_in[0]
        for y in range(1, n_sy):
            value = value + column_in[y]
        whole[i] = value
        for copy in wholes:
            copy.start()

    for at in range(2):
        rims.wait_recv(at)
    for k in range(slabs):
        for part in range(2):
            out[part, k, :b] += up[part, k]
            out[part, k, rows - b :] += down[part, k]
    for at in range(2, len(SIDES)):
        rims.wait_recv(at)
    lane = lax.broadcasted_iota(jnp.int32, (1, n), 1)
    for k in range(slabs):
        for part in range(2):
            for x_ref, y_ref, at, size in ((left, right, 0, rows), (ul, ur, 0, b), (dl, dr, rows - b, b)):
                x, y = x_ref[k], y_ref[k]
                if part == 1:
                    x = pltpu.roll(x, b, 1)
                else:
                    y = pltpu.roll(y, b, 1)
                out[part, k, at : at + size, :n] += jnp.where(lane < b, x, 0.0)
                out[part, k, at : at + size, cols - n :] += jnp.where(lane < b, 0.0, y)

    def whole_arrives(x):
        remote(whole.at[x], whole.at[x], whole_send.at[0], whole_recv.at[x], (x, j, d)).wait_recv()

    for x in across:
        whole_arrives(x)
    pl.when(d > 0)(lambda: whole_arrives(i))
    for x in range(n_sx):
        total_ref[x] = whole[x]

    @pl.when(d == 0)
    def _():
        for copy in parts + columns + wholes:
            copy.wait_send()

    for at in range(len(SIDES)):
        rims.wait_send(at)


VMEM = pl.BlockSpec(memory_space=pltpu.VMEM)
SMEM = pl.BlockSpec(memory_space=pltpu.SMEM)


def call(kernel, args, outs, smem=0, scratch=(), sems=(), collective=None):
    params = dict(vmem_limit_bytes=48 * 1024 * 1024)
    if collective is not None:
        params.update(collective_id=collective, has_side_effects=True)
    return pl.pallas_call(
        kernel,
        out_shape=[jax.ShapeDtypeStruct(shape, F32) for shape in outs],
        in_specs=[SMEM] * smem + [VMEM] * (len(args) - smem),
        out_specs=[VMEM] * len(outs),
        scratch_shapes=[pltpu.VMEM(shape, F32) for shape in scratch]
        + [pltpu.SemaphoreType.DMA(shape) if shape else pltpu.SemaphoreType.DMA for shape in sems],
        compiler_params=pltpu.CompilerParams(**params),
    )(*args)


def local(probe_wave, transmission, scan_offsets, pattern_shifts, patterns):
    n = probe_wave.shape[-1]
    b = n // 2
    _, slabs, rows, cols = transmission.shape
    prop_table, fourier_table = (jnp.asarray(t) for t in build_tables(n))
    offsets = scan_offsets.reshape(-1, 2)
    shifts = pattern_shifts.reshape(-1, 2)
    measured = patterns.reshape(-1, n, n)
    positions = offsets.shape[0]
    n_sx, n_sy, depth = extent()
    probe = jnp.concatenate([probe_wave[0], probe_wave[1]], axis=-1)

    wave_shape = (positions, n, 2 * n)
    store_shape = (positions, slabs, n, 2 * n)
    ext_shape = (2, slabs, rows + n + 8, cols + 2 * n)
    side_shape, edge_shape, corner_shape = (slabs, rows, n), (2, slabs, b, cols), (slabs, b, n)
    rim_shapes = [edge_shape] * 2 + [side_shape] * 2 + [corner_shape] * 4
    chunk = (n // n_sx + 8, 2 * n)
    sides = (len(SIDES),)
    rims = call(halo_kernel, [transmission], rim_shapes, scratch=[side_shape] * 2 + rim_shapes,
                sems=[sides] * 2, collective=0)
    factor, moved = call(
        cut_kernel, [offsets, shifts, transmission, measured, *rims],
        [store_shape, (positions, n, n)], smem=2, scratch=[ext_shape],
    )
    pieces, red = call(
        functools.partial(wave_kernel, 1),
        [factor, probe, moved, prop_table, fourier_table], [store_shape, (n_sx, *chunk)],
        scratch=[store_shape] + [wave_shape] * 4 + [(8, 2 * n)] * 2,
        sems=[(positions,)] * 4 + [()] * 2, collective=2,
    )
    rims = call(scatter_kernel, [offsets, pieces], [transmission.shape, *rim_shapes], smem=1, scratch=[ext_shape])
    transmission_grad, totals = call(
        fold_kernel, [*rims, red], [transmission.shape, (n_sx, *chunk)],
        scratch=rim_shapes + [(n_sx - 1, *chunk), (n_sy, *chunk), chunk, (n_sx, *chunk)],
        sems=[sides] * 2 + [(n_sx - 1,)] * 2 + [(n_sy - 1,), (n_sy,), (n_sx * depth - 1,), (n_sx,)], collective=1,
    )
    all_positions = positions * n_sx * n_sy
    summed = totals[:, : n // n_sx].reshape(n, 2 * n)
    probe_grad = jnp.stack([summed[:, :n], summed[:, n:]]) / all_positions
    mean_error = 0.5 * jnp.sum(totals[0, n // n_sx :, :n]) / (all_positions * n * n)
    return (transmission_grad, probe_grad, mean_error)


def solution(mesh):
    in_specs = (
        P(),
        P(None, "depth", "sx", "sy"),
        P("sx", "sy", None, None),
        P("sx", "sy", None, None),
        P("sx", "sy", None, None, None),
    )
    out_specs = (P(None, "depth", "sx", "sy"), P(), P())
    return jax.shard_map(local, mesh=mesh, in_specs=in_specs, out_specs=out_specs, check_vma=False)
```
